256 devices in a mesh: row: 16 (over z, core), col: 16 (over x, y).
Axes of the slice: x: 4, y: 4, z: 8, core: 2. Of those that a mesh axis runs over, the one named last changes fastest.
Arguments:
- zblock: float32 [65536, 2048], P('row', 'col'), may hold values from -6 to 6
- reflectors: float32 [2, 65536, 256], P(None, 'row'), may hold values from -0.0234375 to 0.0234375
- tfactors: float32 [2, 256, 256], replicated, as said below
Outputs:
- eigvecs: float32 [65536, 2048], P('row', 'col')
The draws below stay inside these ranges and needn't reach their ends.
Inputs may be any that keep to these rules, and one draw needn't show every extreme that they name: Each tfactors[b] is upper triangular with a positive diagonal.
All inputs are finite; a program needn't handle non-finite values.
Results may differ from the reference program's by a relative error of at most 0.0001.
Values sent between devices are 32-bit elements; how exact they have to be, the bound alone decides.
No kernel may reach another device: no remote copies, remote signals or barrier semaphores. Data moves between devices by JAX's collectives and lax.ppermute only.
A program may use at most 64 MiB of HBM per device.

```python
import math
import jax
import jax.numpy as jnp
from jax import lax

K = 2048
BW = 256
ROWS = 65536


def draw_tfactors(key, part):
    key = jax.random.fold_in(key, 7)
    first, second = jax.random.split(key)
    factor = math.sqrt(ROWS * 1.0) / 60.0
    upper = 0.3 * jax.random.normal(first, (2, BW, BW), jnp.float32)
    diag = jax.random.uniform(second, (2, BW), jnp.float32, 1.0, 2.0)
    eye = jnp.eye(BW, dtype=jnp.float32)
    return (jnp.triu(upper, 1) + diag[:, :, None] * eye) * factor


def block_levels(rng, shape, shards, low, high):
    factor_of = 1.0
    for axis_at, shards_of in shards:
        draws = jax.random.uniform(jax.random.fold_in(jax.random.fold_in(rng, 6), axis_at), (shards_of,), jnp.float32, low / len(shards), high / len(shards))
        factor_of = factor_of * jnp.repeat(jnp.exp(draws), shape[axis_at] // shards_of).reshape((-1,) + (1,) * (len(shape) - 1 - axis_at))
    return factor_of


def scatter_about(rng, dims, scale, most, shards=(), held_as=jnp.bfloat16):
    gain = block_levels(rng, dims, shards, -0.22, 0.18) if shards else 1.0
    drawn = jax.random.normal(rng, dims, jnp.float32) * scale * gain
    return jnp.minimum(jnp.maximum(drawn, -most), most).astype(held_as)


def setup_inputs(seed: int = 0) -> dict:
    keys = jax.random.split(jax.random.key(seed), 4)
    zblock = scatter_about(keys[0], (ROWS, K), 1.0, 6.0, ((0, 16), (1, 16)), jnp.float32)
    reflectors = scatter_about(keys[1], (2, ROWS, BW), ROWS ** -0.5, 0.0234375, ((1, 16),), jnp.float32)
    tfactors = draw_tfactors(jax.random.fold_in(keys[3], 71), 0)
    return dict(zblock=zblock, reflectors=reflectors, tfactors=tfactors)


def hdot(left, right):
    return jnp.dot(left, right, precision=lax.Precision.HIGHEST, preferred_element_type=jnp.float32)


def reference(zblock, reflectors, tfactors):
    current = zblock
    for index in (1, 0):
        vblock = reflectors[index]
        product = hdot(vblock.T, current)
        current = current - hdot(vblock, hdot(tfactors[index], product))
    return current
```

```python
import jax
import jax.numpy as jnp
from jax import lax
from jax.sharding import PartitionSpec as P

HIGH = lax.Precision.HIGH


def dot(left, right, dims):
    return lax.dot_general(left, right, ((dims[:1], dims[1:]), ((), ())), precision=HIGH, preferred_element_type=jnp.float32)


def pairs_of(first, second, chips):
    return [(2 * z + core, 2 * (step(z) % chips) + core) for z in range(chips) for core, step in ((0, first), (1, second))]


def aligned(z):
    return z ^ 1


def shifted(z):
    return ((z + 1) ^ 1) - 1


def across(z):
    return z + 3 if z % 2 == 0 else z - 3


def across_back(z):
    return z - 3 if z % 2 == 0 else z + 3


def halves_summed(value, core, swap):
    half = value.shape[0] // 2
    own = lax.dynamic_slice_in_dim(value, core * half, half, 0)
    other = lax.dynamic_slice_in_dim(value, (1 - core) * half, half, 0)
    return own + lax.ppermute(other, "row", swap)


def joined(value, core, swap):
    other = lax.ppermute(value, "row", swap)
    return jnp.where(core == 0, jnp.concatenate([value, other], 0), jnp.concatenate([other, value], 0))


def sums_over_row(values, chips):
    core = lax.axis_index("row") % 2
    swap = [(i, i ^ 1) for i in range(2 * chips)]
    steps = [pairs_of(aligned, shifted, chips), pairs_of(shifted, aligned, chips), pairs_of(across, across_back, chips)]
    parts = [halves_summed(value, core, swap) for value in values]
    for step in steps:
        parts = [part + lax.ppermute(part, "row", step) for part in parts]
    return [joined(part, core, swap) for part in parts]


def body(zblock, reflectors, tfactors):
    v0, v1 = reflectors[0], reflectors[1]
    gram = dot(v0, v1, (0, 0))
    first = dot(v1, zblock, (0, 0))
    second = dot(v0, zblock, (0, 0))
    gram = jnp.concatenate([gram[:, :128], gram[:, 128:]], 0)
    gram, products = sums_over_row([gram, jnp.concatenate([first, second], 0)], 8)
    gram = jnp.concatenate([gram[:256], gram[256:]], 1)
    lead = dot(tfactors[1], products[:256], (1, 0))
    tail = dot(tfactors[0], products[256:] - dot(gram, lead, (1, 0)), (1, 0))
    return zblock - dot(v1, lead, (1, 0)) - dot(v0, tail, (1, 0))


def solution(mesh):
    in_specs = (P("row", "col"), P(None, "row", None), P())
    out_specs = P("row", "col")
    return jax.shard_map(body, mesh=mesh, in_specs=in_specs, out_specs=out_specs, check_vma=False)
```

```python
import functools

import jax
import jax.numpy as jnp
from jax import lax
from jax.experimental import pallas as pl
from jax.experimental.pallas import tpu as pltpu
from jax.sharding import PartitionSpec as P

F32 = jnp.float32
BF16 = jnp.bfloat16
HBM = pl.BlockSpec(memory_space=pl.ANY)
VMEM = pl.BlockSpec(memory_space=pltpu.VMEM)
CHUNKS = 8
MIB = 2**20


def split(value):
    high = value.astype(BF16)
    return high, (value - high.astype(F32)).astype(BF16)


def mm(left, right):
    return jnp.dot(left, right, preferred_element_type=F32)


def exact(left, right, right_dim):
    dims = (((1,), (right_dim,)), ((), ()))
    return lax.dot_general(left, right, dims, precision=lax.Precision.HIGHEST, preferred_element_type=F32)


def call(kernel, ins, outs, scratch, limit, flops):
    cost = pl.CostEstimate(flops=flops, bytes_accessed=4 * MIB, transcendentals=0)
    params = pltpu.CompilerParams(vmem_limit_bytes=limit * MIB)
    specs = [HBM if getattr(shape, "memory_space", None) is None else VMEM for shape in outs]
    return pl.pallas_call(kernel, in_specs=ins, out_specs=specs, out_shape=outs, scratch_shapes=scratch, compiler_params=params, cost_estimate=cost)


def products_kernel(z_hbm, v_hbm, first_ref, second_ref, high_ref, low_ref, z_ref, v_ref, sems):
    rows = z_ref.shape[0] // CHUNKS
    copies = []
    for k in range(CHUNKS):
        part = pl.ds(k * rows, rows)
        group = [pltpu.make_async_copy(z_hbm.at[part], z_ref.at[part], sems.at[k, 2])]
        group += [pltpu.make_async_copy(v_hbm.at[b, part], v_ref.at[b, part], sems.at[k, b]) for b in (1, 0)]
        for copy in group:
            copy.start()
        copies.append(group)
    totals = [None, None]
    for k in range(CHUNKS):
        part = pl.ds(k * rows, rows)
        for copy in copies[k]:
            copy.wait()
        z_high, z_low = split(z_ref[part, :].T)
        z_both = jnp.concatenate([z_high, z_low], 0)
        for b in (1, 0):
            high, low = split(v_ref[b, part, :])
            high_ref[b, part, :] = high
            low_ref[b, part, :] = low
            both = mm(z_both, high)
            term = both[:128] + both[128:] + mm(z_high, low)
            totals[b] = term if k == 0 else totals[b] + term
    first_ref[...] = totals[1]
    second_ref[...] = totals[0]


def gram_kernel(high_ref, low_ref, upper_ref, lower_ref):
    rows = high_ref.shape[1] // CHUNKS
    total = None
    for k in range(CHUNKS):
        part = pl.ds(k * rows, rows)
        left = jnp.concatenate([high_ref[1, part, :].T, low_ref[1, part, :].T], 0)
        both = mm(left, high_ref[0, part, :])
        term = both[:256] + both[256:] + mm(left[:256], low_ref[0, part, :])
        total = term if k == 0 else total + term
    upper_ref[...] = total[:128]
    lower_ref[...] = total[128:]


def widened(value):
    return jnp.concatenate(split(value.T), 1)


def updated(base, high, low, wide):
    both = mm(high, wide) + mm(low, wide)
    return base - (both[:, :128] + both[:, 128:])


def lead_kernel(z_ref, high_ref, low_ref, t_ref, first_ref, lead_ref, base_ref):
    lead = exact(first_ref[...], t_ref[1], 1)
    lead_ref[...] = lead
    wide = widened(lead)
    rows = z_ref.shape[0] // CHUNKS
    for k in range(CHUNKS):
        part = pl.ds(k * rows, rows)
        base_ref[part, :] = updated(z_ref[part, :], high_ref[1, part, :], low_ref[1, part, :], wide)


def tail_kernel(base_ref, high_ref, low_ref, t_ref, lead_ref, second_ref, gram_ref, out_hbm, out_ref, sems):
    tail = exact(second_ref[...] - exact(lead_ref[...], gram_ref[...], 0), t_ref[0], 1)
    wide = widened(tail)
    rows = base_ref.shape[0] // CHUNKS
    copies = []
    for k in range(CHUNKS):
        part = pl.ds(k * rows, rows)
        out_ref[part, :] = updated(base_ref[part, :], high_ref[0, part, :], low_ref[0, part, :], wide)
        copy = pltpu.make_async_copy(out_ref.at[part], out_hbm.at[part], sems.at[k])
        copy.start()
        copies.append(copy)
    for copy in copies:
        copy.wait()


def pairs_of(first, second, chips):
    return [(2 * z + core, 2 * (step(z) % chips) + core) for z in range(chips) for core, step in ((0, first), (1, second))]


def aligned(z):
    return z ^ 1


def shifted(z):
    return ((z + 1) ^ 1) - 1


def across(z):
    return z + 3 if z % 2 == 0 else z - 3


def across_back(z):
    return z - 3 if z % 2 == 0 else z + 3


def sums_over_row(pairs, chips):
    even = lax.axis_index("row") % 2 == 0
    swap = [(i, i ^ 1) for i in range(2 * chips)]
    steps = [pairs_of(aligned, shifted, chips), pairs_of(shifted, aligned, chips), pairs_of(across, across_back, chips)]
    parts = [jnp.where(even, one, two) + lax.ppermute(jnp.where(even, two, one), "row", swap) for one, two in pairs]
    for step in steps:
        parts = [part + lax.ppermute(part, "row", step) for part in parts]
    results = []
    for part in parts:
        other = lax.ppermute(part, "row", swap)
        results.append((jnp.where(even, part, other), jnp.where(even, other, part)))
    return results


def body(zblock, reflectors, tfactors):
    rows, columns = zblock.shape
    width = reflectors.shape[2]
    product = pltpu.VMEM((columns, width), F32)
    halves = pltpu.VMEM(reflectors.shape, BF16)
    whole = pltpu.VMEM(zblock.shape, F32)
    work = 6 * rows * columns * width
    first, second, high, low, zblock = call(
        products_kernel,
        [HBM, HBM],
        [product, product, halves, halves, whole],
        [pltpu.VMEM(reflectors.shape, F32), pltpu.SemaphoreType.DMA((CHUNKS, 3))],
        44,
        2 * work,
    )(zblock, reflectors)
    upper, lower = call(gram_kernel, [VMEM] * 2, [product, product], [], 16, 2 * work)(high, low)
    (first, second), (upper, lower) = sums_over_row([(first, second), (upper, lower)], 8)
    lead, base = call(lead_kernel, [VMEM] * 5, [product, whole], [], 16, work)(zblock, high, low, tfactors, first)
    gram = jnp.concatenate([upper, lower], 0)
    result = jax.ShapeDtypeStruct(zblock.shape, F32)
    scratch = [whole, pltpu.SemaphoreType.DMA((CHUNKS,))]
    return call(tail_kernel, [VMEM] * 7, [result], scratch, 16, work)(base, high, low, tfactors, lead, second, gram)[0]


def solution(mesh):
    in_specs = (P("row", "col"), P(None, "row", None), P())
    out_specs = P("row", "col")
    return jax.shard_map(body, mesh=mesh, in_specs=in_specs, out_specs=out_specs, check_vma=False)
```

```python
import functools

import jax
import jax.numpy as jnp
from jax import lax
from jax.experimental import pallas as pl
from jax.experimental.pallas import tpu as pltpu
from jax.sharding import PartitionSpec as P

F32 = jnp.float32
BF16 = jnp.bfloat16
HBM = pl.BlockSpec(memory_space=pl.ANY)
VMEM = pl.BlockSpec(memory_space=pltpu.VMEM)
CHUNKS = 8
OUT_CHUNKS = 16
MIB = 2**20


def split(value):
    high = value.astype(BF16)
    return high, (value - high.astype(F32)).astype(BF16)


def mm(left, right):
    return jnp.dot(left, right, preferred_element_type=F32)


def small(left, right, right_dim):
    dims = (((1,), (right_dim,)), ((), ()))
    left_high, left_low = split(left)
    right_high, right_low = split(right)
    rows = left.shape[0]
    both = lax.dot_general(jnp.concatenate([left_high, left_low], 0), right_high, dims, preferred_element_type=F32)
    return both[:rows] + both[rows:] + lax.dot_general(left_high, right_low, dims, preferred_element_type=F32)


def call(kernel, ins, outs, scratch, limit, flops):
    cost = pl.CostEstimate(flops=flops, bytes_accessed=4 * MIB, transcendentals=0)
    params = pltpu.CompilerParams(vmem_limit_bytes=limit * MIB)
    specs = [HBM if getattr(shape, "memory_space", None) is None else VMEM for shape in outs]
    return pl.pallas_call(kernel, in_specs=ins, out_specs=specs, out_shape=outs, scratch_shapes=scratch, compiler_params=params, cost_estimate=cost)


def products_kernel(z_hbm, v_hbm, first_ref, second_ref, high_ref, low_ref, z_ref, v_ref, sems):
    rows = z_ref.shape[0] // CHUNKS
    copies = []
    for k in range(CHUNKS):
        part = pl.ds(k * rows, rows)
        group = [pltpu.make_async_copy(z_hbm.at[part], z_ref.at[part], sems.at[k, 2])]
        group += [pltpu.make_async_copy(v_hbm.at[b, part], v_ref.at[b, part], sems.at[k, b]) for b in (1, 0)]
        for copy in group:
            copy.start()
        copies.append(group)
    totals = [None, None]
    for k in range(CHUNKS):
        part = pl.ds(k * rows, rows)
        for copy in copies[k]:
            copy.wait()
        z_high, z_low = split(z_ref[part, :].T)
        z_both = jnp.concatenate([z_high, z_low], 0)
        for b in (1, 0):
            high, low = split(v_ref[b, part, :])
            high_ref[b, part, :] = high
            low_ref[b, part, :] = low
            both = mm(z_both, high)
            term = both[:128] + both[128:] + mm(z_high, low)
            totals[b] = term if k == 0 else totals[b] + term
    first_ref[...] = totals[1]
    second_ref[...] = totals[0]


def gram_kernel(high_ref, low_ref, after_hbm, upper_ref, lower_ref):
    rows = high_ref.shape[1] // CHUNKS
    total = None
    for k in range(CHUNKS):
        part = pl.ds(k * rows, rows)
        left = jnp.concatenate([high_ref[1, part, :].T, low_ref[1, part, :].T], 0)
        both = mm(left, high_ref[0, part, :])
        term = both[:256] + both[256:] + mm(left[:256], low_ref[0, part, :])
        total = term if k == 0 else total + term
    upper_ref[...] = total[:128]
    lower_ref[...] = total[128:]


def widened(value):
    return jnp.concatenate(split(value.T), 1)


def updated(base, high, low, wide):
    both = mm(high, wide) + mm(low, wide)
    return base - (both[:, :128] + both[:, 128:])


def lead_kernel(z_ref, high_ref, low_ref, t_ref, first_ref, lead_ref, base_ref):
    lead = small(first_ref[...], t_ref[1], 1)
    lead_ref[...] = lead
    wide = widened(lead)
    rows = z_ref.shape[0] // CHUNKS
    for k in range(CHUNKS):
        part = pl.ds(k * rows, rows)
        base_ref[part, :] = updated(z_ref[part, :], high_ref[1, part, :], low_ref[1, part, :], wide)


def tail_kernel(base_ref, high_ref, low_ref, t_ref, lead_ref, second_ref, gram_ref, out_hbm, out_ref, sems):
    tail = small(second_ref[...] - small(lead_ref[...], gram_ref[...], 0), t_ref[0], 1)
    wide = widened(tail)
    rows = base_ref.shape[0] // OUT_CHUNKS
    copies = []
    for k in range(OUT_CHUNKS):
        part = pl.ds(k * rows, rows)
        out_ref[part, :] = updated(base_ref[part, :], high_ref[0, part, :], low_ref[0, part, :], wide)
        copy = pltpu.make_async_copy(out_ref.at[part], out_hbm.at[part], sems.at[k])
        copy.start()
        copies.append(copy)
    for copy in copies:
        copy.wait()


def pairs_of(first, second, chips):
    return [(2 * z + core, 2 * (step(z) % chips) + core) for z in range(chips) for core, step in ((0, first), (1, second))]


def aligned(z):
    return z ^ 1


def shifted(z):
    return ((z + 1) ^ 1) - 1


def across(z):
    return z + 3 if z % 2 == 0 else z - 3


def across_back(z):
    return z - 3 if z % 2 == 0 else z + 3


CHIPS = 8
SWAP = [(i, i ^ 1) for i in range(2 * CHIPS)]
STEPS = [pairs_of(aligned, shifted, CHIPS), pairs_of(shifted, aligned, CHIPS), pairs_of(across, across_back, CHIPS)]


def half_sum(one, two):
    even = lax.axis_index("row") % 2 == 0
    return jnp.where(even, one, two) + lax.ppermute(jnp.where(even, two, one), "row", SWAP)


def sum_along_z(part):
    for step in STEPS:
        part = part + lax.ppermute(part, "row", step)
    return part


def both_halves(part):
    even = lax.axis_index("row") % 2 == 0
    other = lax.ppermute(part, "row", SWAP)
    return jnp.where(even, part, other), jnp.where(even, other, part)


def body(zblock, reflectors, tfactors):
    rows, columns = zblock.shape
    width = reflectors.shape[2]
    product = pltpu.VMEM((columns, width), F32)
    halves = pltpu.VMEM(reflectors.shape, BF16)
    whole = pltpu.VMEM(zblock.shape, F32)
    work = 6 * rows * columns * width
    first, second, high, low, zblock = call(
        products_kernel,
        [HBM, HBM],
        [product, product, halves, halves, whole],
        [pltpu.VMEM(reflectors.shape, F32), pltpu.SemaphoreType.DMA((CHUNKS, 3))],
        44,
        2 * work,
    )(zblock, reflectors)
    part = half_sum(first, second)
    upper, lower = call(gram_kernel, [VMEM, VMEM, HBM], [product, product], [], 16, 2 * work)(high, low, part)
    gram_part = half_sum(upper, lower)
    first, second = both_halves(sum_along_z(part))
    upper, lower = both_halves(sum_along_z(gram_part))
    lead, base = call(lead_kernel, [VMEM] * 5, [product, whole], [], 16, work)(zblock, high, low, tfactors, first)
    gram = jnp.concatenate([upper, lower], 0)
    result = jax.ShapeDtypeStruct(zblock.shape, F32)
    scratch = [whole, pltpu.SemaphoreType.DMA((OUT_CHUNKS,))]
    return call(tail_kernel, [VMEM] * 7, [result], scratch, 16, work)(base, high, low, tfactors, lead, second, gram)[0]


def solution(mesh):
    in_specs = (P("row", "col"), P(None, "row", None), P())
    out_specs = P("row", "col")
    return jax.shard_map(body, mesh=mesh, in_specs=in_specs, out_specs=out_specs, check_vma=False)
```

```python
import functools

import jax
import jax.numpy as jnp
from jax import lax
from jax.experimental import pallas as pl
from jax.experimental.pallas import tpu as pltpu
from jax.sharding import PartitionSpec as P

F32 = jnp.float32
BF16 = jnp.bfloat16
HBM = pl.BlockSpec(memory_space=pl.ANY)
VMEM = pl.BlockSpec(memory_space=pltpu.VMEM)
CHUNKS = 8
OUT_CHUNKS = 16
MIB = 2**20


def split(value):
    high = value.astype(BF16)
    return high, (value - high.astype(F32)).astype(BF16)


def mm(left, right):
    return jnp.dot(left, right, preferred_element_type=F32)


def small(left, right, right_dim):
    dims = (((1,), (right_dim,)), ((), ()))
    left_high, left_low = split(left)
    right_high, right_low = split(right)
    rows = left.shape[0]
    both = lax.dot_general(jnp.concatenate([left_high, left_low], 0), right_high, dims, preferred_element_type=F32)
    return both[:rows] + both[rows:] + lax.dot_general(left_high, right_low, dims, preferred_element_type=F32)


def call(kernel, ins, outs, scratch, limit, flops):
    cost = pl.CostEstimate(flops=flops, bytes_accessed=4 * MIB, transcendentals=0)
    params = pltpu.CompilerParams(vmem_limit_bytes=limit * MIB)
    specs = [HBM if getattr(shape, "memory_space", None) is None else VMEM for shape in outs]
    return pl.pallas_call(kernel, in_specs=ins, out_specs=specs, out_shape=outs, scratch_shapes=scratch, compiler_params=params, cost_estimate=cost)


def products_kernel(z_hbm, v_hbm, first_ref, second_ref, high_ref, low_ref, z_ref, v_ref, sems):
    rows = z_ref.shape[0] // CHUNKS
    copies = []
    for k in range(CHUNKS):
        part = pl.ds(k * rows, rows)
        group = [pltpu.make_async_copy(z_hbm.at[part], z_ref.at[part], sems.at[k, 2])]
        group += [pltpu.make_async_copy(v_hbm.at[b, part], v_ref.at[b, part], sems.at[k, b]) for b in (1, 0)]
        for copy in group:
            copy.start()
        copies.append(group)
    totals = [None, None]
    for k in range(CHUNKS):
        part = pl.ds(k * rows, rows)
        for copy in copies[k]:
            copy.wait()
        z_high, z_low = split(z_ref[part, :].T)
        z_both = jnp.concatenate([z_high, z_low], 0)
        for b in (1, 0):
            high, low = split(v_ref[b, part, :])
            high_ref[b, part, :] = high
            low_ref[b, part, :] = low
            both = mm(z_both, high)
            term = both[:128] + both[128:] + mm(z_high, low)
            totals[b] = term if k == 0 else totals[b] + term
    first_ref[...] = totals[1]
    second_ref[...] = totals[0]


def gram_kernel(high_ref, low_ref, upper_ref, lower_ref):
    rows = high_ref.shape[1] // CHUNKS
    total = None
    for k in range(CHUNKS):
        part = pl.ds(k * rows, rows)
        left = jnp.concatenate([high_ref[1, part, :].T, low_ref[1, part, :].T], 0)
        both = mm(left, high_ref[0, part, :])
        term = both[:256] + both[256:] + mm(left[:256], low_ref[0, part, :])
        total = term if k == 0 else total + term
    upper_ref[...] = total[:128]
    lower_ref[...] = total[128:]


def widened(value):
    return jnp.concatenate(split(value.T), 1)


def updated(base, high, low, wide):
    both = mm(high, wide) + mm(low, wide)
    return base - (both[:, :128] + both[:, 128:])


def lead_kernel(z_ref, high_ref, low_ref, t_ref, first_ref, lead_ref, base_ref):
    lead = small(first_ref[...], t_ref[1], 1)
    lead_ref[...] = lead
    wide = widened(lead)
    rows = z_ref.shape[0] // CHUNKS
    for k in range(CHUNKS):
        part = pl.ds(k * rows, rows)
        base_ref[part, :] = updated(z_ref[part, :], high_ref[1, part, :], low_ref[1, part, :], wide)


def tail_kernel(base_ref, high_ref, low_ref, t_ref, lead_ref, second_ref, gram_ref, out_hbm, out_ref, sems):
    tail = small(second_ref[...] - small(lead_ref[...], gram_ref[...], 0), t_ref[0], 1)
    wide = widened(tail)
    rows = base_ref.shape[0] // OUT_CHUNKS
    copies = []
    for k in range(OUT_CHUNKS):
        part = pl.ds(k * rows, rows)
        out_ref[part, :] = updated(base_ref[part, :], high_ref[0, part, :], low_ref[0, part, :], wide)
        copy = pltpu.make_async_copy(out_ref.at[part], out_hbm.at[part], sems.at[k])
        copy.start()
        copies.append(copy)
    for copy in copies:
        copy.wait()


def pairs_of(first, second, chips):
    return [(2 * z + core, 2 * (step(z) % chips) + core) for z in range(chips) for core, step in ((0, first), (1, second))]


def aligned(z):
    return z ^ 1


def shifted(z):
    return ((z + 1) ^ 1) - 1


def across(z):
    return z + 3 if z % 2 == 0 else z - 3


def across_back(z):
    return z - 3 if z % 2 == 0 else z + 3


CHIPS = 8
SWAP = [(i, i ^ 1) for i in range(2 * CHIPS)]
STEPS = [pairs_of(aligned, shifted, CHIPS), pairs_of(shifted, aligned, CHIPS), pairs_of(across, across_back, CHIPS)]
TURNED = [pairs_of(shifted, aligned, CHIPS), pairs_of(aligned, shifted, CHIPS), pairs_of(across_back, across, CHIPS)]


def half_sum(one, two):
    even = lax.axis_index("row") % 2 == 0
    return jnp.where(even, one, two) + lax.ppermute(jnp.where(even, two, one), "row", SWAP)


def sum_along_z(part, steps):
    for step in steps:
        part = part + lax.ppermute(part, "row", step)
    return part


def both_halves(part):
    even = lax.axis_index("row") % 2 == 0
    other = lax.ppermute(part, "row", SWAP)
    return jnp.where(even, part, other), jnp.where(even, other, part)


def body(zblock, reflectors, tfactors):
    rows, columns = zblock.shape
    width = reflectors.shape[2]
    product = pltpu.VMEM((columns, width), F32)
    halves = pltpu.VMEM(reflectors.shape, BF16)
    whole = pltpu.VMEM(zblock.shape, F32)
    work = 6 * rows * columns * width
    first, second, high, low, zblock = call(
        products_kernel,
        [HBM, HBM],
        [product, product, halves, halves, whole],
        [pltpu.VMEM(reflectors.shape, F32), pltpu.SemaphoreType.DMA((CHUNKS, 3))],
        44,
        2 * work,
    )(zblock, reflectors)
    part = half_sum(first, second)
    upper, lower = call(gram_kernel, [VMEM, VMEM], [product, product], [], 16, 2 * work)(high, low)
    _, upper, lower = lax.optimization_barrier((part, upper, lower))
    gram_part = half_sum(upper, lower)
    first, second = both_halves(sum_along_z(part, STEPS))
    upper, lower = both_halves(sum_along_z(gram_part, TURNED))
    lead, base = call(lead_kernel, [VMEM] * 5, [product, whole], [], 16, work)(zblock, high, low, tfactors, first)
    gram = jnp.concatenate([upper, lower], 0)
    result = jax.ShapeDtypeStruct(zblock.shape, F32)
    scratch = [whole, pltpu.SemaphoreType.DMA((OUT_CHUNKS,))]
    return call(tail_kernel, [VMEM] * 7, [result], scratch, 16, work)(base, high, low, tfactors, lead, second, gram)[0]


def solution(mesh):
    in_specs = (P("row", "col"), P(None, "row", None), P())
    out_specs = P("row", "col")
    return jax.shard_map(body, mesh=mesh, in_specs=in_specs, out_specs=out_specs, check_vma=False)
```

```python
import functools

import jax
import jax.numpy as jnp
from jax import lax
from jax.experimental import pallas as pl
from jax.experimental.pallas import tpu as pltpu
from jax.sharding import PartitionSpec as P

F32 = jnp.float32
BF16 = jnp.bfloat16
HBM = pl.BlockSpec(memory_space=pl.ANY)
VMEM = pl.BlockSpec(memory_space=pltpu.VMEM)
CHUNKS = 8
OUT_CHUNKS = 16
MIB = 2**20


def split(value):
    high = value.astype(BF16)
    return high, (value - high.astype(F32)).astype(BF16)


def mm(left, right):
    return jnp.dot(left, right, preferred_element_type=F32)


def small(left, right, right_dim):
    dims = (((1,), (right_dim,)), ((), ()))
    left_high, left_low = split(left)
    right_high, right_low = split(right)
    rows = left.shape[0]
    both = lax.dot_general(jnp.concatenate([left_high, left_low], 0), right_high, dims, preferred_element_type=F32)
    return both[:rows] + both[rows:] + lax.dot_general(left_high, right_low, dims, preferred_element_type=F32)


def call(kernel, ins, outs, scratch, limit, flops):
    cost = pl.CostEstimate(flops=flops, bytes_accessed=4 * MIB, transcendentals=0)
    params = pltpu.CompilerParams(vmem_limit_bytes=limit * MIB)
    specs = [HBM if getattr(shape, "memory_space", None) is None else VMEM for shape in outs]
    return pl.pallas_call(kernel, in_specs=ins, out_specs=specs, out_shape=outs, scratch_shapes=scratch, compiler_params=params, cost_estimate=cost)


def products_kernel(z_hbm, v_hbm, first_ref, second_ref, high_ref, low_ref, z_ref, v_ref, sems):
    rows = z_ref.shape[0] // CHUNKS
    copies = []
    for k in range(CHUNKS):
        part = pl.ds(k * rows, rows)
        group = [pltpu.make_async_copy(z_hbm.at[part], z_ref.at[part], sems.at[k, 2])]
        group += [pltpu.make_async_copy(v_hbm.at[b, part], v_ref.at[b, part], sems.at[k, b]) for b in (1, 0)]
        for copy in group:
            copy.start()
        copies.append(group)
    totals = [None, None]
    for k in range(CHUNKS):
        part = pl.ds(k * rows, rows)
        for copy in copies[k]:
            copy.wait()
        z_high, z_low = split(z_ref[part, :].T)
        z_both = jnp.concatenate([z_high, z_low], 0)
        for b in (1, 0):
            high, low = split(v_ref[b, part, :])
            high_ref[b, part, :] = high
            low_ref[b, part, :] = low
            both = mm(z_both, high)
            term = both[:128] + both[128:] + mm(z_high, low)
            totals[b] = term if k == 0 else totals[b] + term
    first_ref[...] = totals[1]
    second_ref[...] = totals[0]


def gram_kernel(high_ref, low_ref, upper_ref, lower_ref):
    rows = high_ref.shape[1] // CHUNKS
    total = None
    for k in range(CHUNKS):
        part = pl.ds(k * rows, rows)
        left = jnp.concatenate([high_ref[1, part, :].T, low_ref[1, part, :].T], 0)
        both = mm(left, high_ref[0, part, :])
        term = both[:256] + both[256:] + mm(left[:256], low_ref[0, part, :])
        total = term if k == 0 else total + term
    upper_ref[...] = total[:128]
    lower_ref[...] = total[128:]


def widened(value):
    return jnp.concatenate(split(value.T), 1)


def updated(base, high, low, wide):
    both = mm(high, wide)
    return base - (both[:, :128] + (both[:, 128:] + mm(low, wide[:, :128])))


def lead_kernel(z_ref, high_ref, low_ref, t_ref, first_ref, lead_ref, base_ref):
    lead = small(first_ref[...], t_ref[1], 1)
    lead_ref[...] = lead
    wide = widened(lead)
    rows = z_ref.shape[0] // CHUNKS
    for k in range(CHUNKS):
        part = pl.ds(k * rows, rows)
        base_ref[part, :] = updated(z_ref[part, :], high_ref[1, part, :], low_ref[1, part, :], wide)


def tail_kernel(base_ref, high_ref, low_ref, t_ref, lead_ref, second_ref, gram_ref, out_hbm, out_ref, sems):
    tail = small(second_ref[...] - small(lead_ref[...], gram_ref[...], 0), t_ref[0], 1)
    wide = widened(tail)
    rows = base_ref.shape[0] // OUT_CHUNKS
    copies = []
    for k in range(OUT_CHUNKS):
        part = pl.ds(k * rows, rows)
        out_ref[part, :] = updated(base_ref[part, :], high_ref[0, part, :], low_ref[0, part, :], wide)
        copy = pltpu.make_async_copy(out_ref.at[part], out_hbm.at[part], sems.at[k])
        copy.start()
        copies.append(copy)
    for copy in copies:
        copy.wait()


def pairs_of(first, second, chips):
    return [(2 * z + core, 2 * (step(z) % chips) + core) for z in range(chips) for core, step in ((0, first), (1, second))]


def aligned(z):
    return z ^ 1


def shifted(z):
    return ((z + 1) ^ 1) - 1


def across(z):
    return z + 3 if z % 2 == 0 else z - 3


def across_back(z):
    return z - 3 if z % 2 == 0 else z + 3


CHIPS = 8
SWAP = [(i, i ^ 1) for i in range(2 * CHIPS)]
STEPS = [pairs_of(aligned, shifted, CHIPS), pairs_of(shifted, aligned, CHIPS), pairs_of(across, across_back, CHIPS)]
TURNED = [pairs_of(shifted, aligned, CHIPS), pairs_of(aligned, shifted, CHIPS), pairs_of(across_back, across, CHIPS)]


def half_sum(one, two):
    even = lax.axis_index("row") % 2 == 0
    return jnp.where(even, one, two) + lax.ppermute(jnp.where(even, two, one), "row", SWAP)


def sum_along_z(part, steps):
    for step in steps:
        part = part + lax.ppermute(part, "row", step)
    return part


def both_halves(part):
    even = lax.axis_index("row") % 2 == 0
    other = lax.ppermute(part, "row", SWAP)
    return jnp.where(even, part, other), jnp.where(even, other, part)


def body(zblock, reflectors, tfactors):
    rows, columns = zblock.shape
    width = reflectors.shape[2]
    product = pltpu.VMEM((columns, width), F32)
    halves = pltpu.VMEM(reflectors.shape, BF16)
    whole = pltpu.VMEM(zblock.shape, F32)
    work = 6 * rows * columns * width
    first, second, high, low, zblock = call(
        products_kernel,
        [HBM, HBM],
        [product, product, halves, halves, whole],
        [pltpu.VMEM(reflectors.shape, F32), pltpu.SemaphoreType.DMA((CHUNKS, 3))],
        44,
        2 * work,
    )(zblock, reflectors)
    part = half_sum(first, second)
    upper, lower = call(gram_kernel, [VMEM, VMEM], [product, product], [], 16, 2 * work)(high, low)
    _, upper, lower = lax.optimization_barrier((part, upper, lower))
    gram_part = half_sum(upper, lower)
    first, second = both_halves(sum_along_z(part, STEPS))
    upper, lower = both_halves(sum_along_z(gram_part, TURNED))
    lead, base = call(lead_kernel, [VMEM] * 5, [product, whole], [], 16, work)(zblock, high, low, tfactors, first)
    gram = jnp.concatenate([upper, lower], 0)
    result = jax.ShapeDtypeStruct(zblock.shape, F32)
    scratch = [whole, pltpu.SemaphoreType.DMA((OUT_CHUNKS,))]
    return call(tail_kernel, [VMEM] * 7, [result], scratch, 16, work)(base, high, low, tfactors, lead, second, gram)[0]


def solution(mesh):
    in_specs = (P("row", "col"), P(None, "row", None), P())
    out_specs = P("row", "col")
    return jax.shard_map(body, mesh=mesh, in_specs=in_specs, out_specs=out_specs, check_vma=False)
```
